32 devices in a mesh: dp: 2 (over core), ctx: 8 (over z, y), exp: 2 (over x).
Axes of the slice: x: 2, y: 2, z: 4, core: 2. Of those that a mesh axis runs over, the one named last changes fastest.
Arguments:
- tokens: bfloat16 [2, 1024, 2560], P('dp', 'ctx'), may hold values from -6 to 6
- queries: bfloat16 [2, 1024, 16, 576], P('dp', 'ctx', 'exp'), may hold values from -240 to 240
- kv_weight: bfloat16 [2560, 576], P('exp'), may hold values from -0.125 to 0.125
- kv_gain: bfloat16 [512], replicated, may hold values from 0.5 to 1.5
- uv_weight: bfloat16 [16, 512, 128], P('exp'), may hold values from -0.75 to 0.75
- out_weight: bfloat16 [2048, 2560], P('exp'), may hold values from -0.5 to 0.5
- post_gain: bfloat16 [2560], replicated, may hold values from 0.5 to 1.5
- router_weight: bfloat16 [2560, 16], replicated, may hold values from -0.125 to 0.125
- expert_ids: int32 [2, 1024, 6], P('dp', 'ctx'), may hold values from 0 to 15, all different within a row; in each aligned block of 128 rows (0 to 127, 128 to 255, ..., all dimensions but the last counted through in order) at most 64 rows name the same one
- doc_ids: int32 [2, 1024], P('dp', 'ctx'), may hold values from 0 to 3, never falling along the last dimension, each value on 1 to 512 neighbouring positions
- gate_weight: bfloat16 [16, 2560, 1536], P('ctx', None, 'exp'), may hold values from -0.125 to 0.125
- up_weight: bfloat16 [16, 2560, 1536], P('ctx', None, 'exp'), may hold values from -0.125 to 0.125
- down_weight: bfloat16 [16, 1536, 2560], P('ctx', 'exp'), may hold values from -0.15625 to 0.15625
- cotangent: bfloat16 [2, 1024, 2560], P('dp', 'ctx'), may hold values from -6 to 6
Outputs:
- layer_out: bfloat16 [2, 1024, 2560], P('dp', 'ctx')
- router_grad: float32 [2560, 16], replicated
- gate_grad: bfloat16 [16, 2560, 1536], P('ctx', 'dp', 'exp')
- up_grad: bfloat16 [16, 2560, 1536], P('ctx', 'dp', 'exp')
- down_grad: bfloat16 [16, 1536, 2560], P('ctx', 'exp', 'dp')
The draws below stay inside these ranges and needn't reach their ends.
Inputs may be any that keep to these rules, and one draw needn't show every extreme that they name: `expert_ids`: in each aligned block of 128 positions of a sequence no expert is named by more than 64 of the block's assignments; the experts of one token differ. `doc_ids`: document numbers never fall along a sequence; a document has at most 512 positions.
All inputs are finite; a program needn't handle non-finite values.
Results may differ from the reference program's by a relative error of at most 0.023.
The reference program's roundings to bfloat16 on the way count: a program that leaves them out, or rounds other values in their place, can miss the bound.
Values may be sent and summed in bfloat16 or wider, within the bound.
A program may use at most 192 MiB of HBM per device.

```python
import math
import jax
import jax.numpy as jnp
import numpy as np
from jax import lax

D = 2560
HEADS = 16
LAT = 512
ROPE = 64
NOPE = 128
VH = 128
FFE = 1536
TOPK = 6
DOCS = 4
SEQ_DEV = 128
BATCH = 2
SEQ = 1024
EXPERTS = 16
CAP = 64
N_CTX = 8
N_EXP = 2


def draw_queries(key, part):
    first_key = jax.random.fold_in(jax.random.fold_in(key, 11), 0)
    shape = (BATCH, SEQ, HEADS, LAT + ROPE)
    base = jnp.clip(jax.random.normal(first_key, shape, jnp.float32), -6.0, 6.0)
    return base.astype(jnp.bfloat16)


def shard_levels(key, dims, cuts, low, top_value):
    factor_of = 1.0
    for dim, blocks in cuts:
        steps = jax.random.uniform(jax.random.fold_in(jax.random.fold_in(key, 6), dim), (blocks,), jnp.float32, low / len(cuts), top_value / len(cuts))
        factor_of = factor_of * jnp.repeat(jnp.exp(steps), dims[dim] // blocks).reshape((-1,) + (1,) * (len(dims) - 1 - dim))
    return factor_of


def profile(number_of, total, limit, lean):
    loads = [(1 << 20) // math.isqrt(grade ** lean) + 1 for grade in range(2, number_of + 1)]
    surplus, holding = total - limit - (number_of - 1), [1] * (number_of - 1)
    while surplus > 0:
        free = [i for i in range(number_of - 1) if holding[i] < limit]
        mass, remaining = sum([loads[i] for i in free]), surplus
        for i in free:
            addition = min(limit - holding[i], max(1, remaining * loads[i] // mass), surplus)
            holding[i] = holding[i] + addition
            surplus = surplus - addition
    return np.array([limit] + holding)


def ragged_sizes(own_key, count, total, limit, skew):
    if count == 2:
        one = jax.random.randint(own_key, (), max(1, total - limit), min(limit, total - 1) + 1)
        return jnp.stack([one, total - one])
    sizes = jnp.asarray(profile(count, total, limit, skew), jnp.int32)
    pairs = (count - 1) // 2
    source_of, sink = sizes[1:1 + 2 * pairs:2], sizes[2:2 + 2 * pairs:2]
    room = jnp.minimum(source_of - 1, limit - sink)
    passed = jax.random.randint(jax.random.fold_in(own_key, 1), (pairs,), 0, 1 << 20) % (room + 1)
    sizes = sizes.at[1:1 + 2 * pairs:2].set(source_of - passed).at[2:2 + 2 * pairs:2].set(sink + passed)
    return sizes[jax.random.permutation(jax.random.fold_in(own_key, 2), count)]


def assign_block(key, own, number, rows, amount, top, limit, slope):
    sequence = jax.random.permutation(key, amount)
    crowded, usual = shares(amount, rows * top, limit, slope, True), shares(amount, rows * top, limit, slope, False)
    places = jnp.arange(amount)

    def named(lengths, turn):
        used = int((lengths > 0).sum())
        fixed = max(1, used // 4)
        passed = fixed + (places - fixed + turn * (used - fixed)) % max(1, amount - fixed)
        return jnp.zeros((amount,), jnp.int32).at[sequence[jnp.where(places < fixed, places, passed)]].set(jnp.asarray(lengths, jnp.int32))

    lengths = jnp.where(number % 4 == 0, named(crowded, number // 4), named(usual, number - number // 4 - 1))
    mixed = jax.random.permutation(jax.random.fold_in(own, 3), amount)
    giver, taker = mixed[0:amount // 2 * 2:2], mixed[1:amount // 2 * 2:2]
    margin = jnp.minimum(lengths[giver] - 1, limit - lengths[taker]) // 2
    margin = jnp.where((giver == sequence[0]) | (taker == sequence[0]) | (lengths[taker] == 0), 0, jnp.maximum(margin, 0))
    passed = jax.random.randint(jax.random.fold_in(own, 4), (amount // 2,), 0, 1 << 20) % (margin + 1)
    lengths = lengths.at[giver].add(-passed).at[taker].add(passed)
    members = jnp.searchsorted(jnp.cumsum(lengths), jnp.arange(rows * top), side="right").astype(jnp.int32)
    listing = members.reshape(top, rows).T
    listing = listing[jax.random.permutation(jax.random.fold_in(own, 1), rows)]
    turn = jax.random.randint(jax.random.fold_in(own, 2), (rows, 1), 0, top)
    return jnp.take_along_axis(listing, (jnp.arange(top)[None, :] + turn) % top, axis=1)


def shares(count, total, most, slope, full):
    weights = [(1 << 20) // math.isqrt(grade ** slope) + 1 for grade in range(1, count + 1)]
    largest = most if full else min(most, max(-(-total // count), total * weights[0] // sum(weights)))
    least = 1 if total - largest >= count - 1 else 0
    given, spare = [largest] + [least] * (count - 1), total - largest - least * (count - 1)
    while spare > 0:
        free = [i for i in range(1, count) if given[i] < largest] or [i for i in range(1, count) if given[i] < most]
        whole, left = sum([weights[i] for i in free]), spare
        for i in free:
            addition = min(most - given[i], max(1, left * weights[i] // whole), spare)
            given[i] = given[i] + addition
            spare = spare - addition
    return np.array(given)


def scatter_about(stream_key, shape, scale, limit, cuts=(), kind=jnp.bfloat16):
    level = shard_levels(stream_key, shape, cuts, -0.22, 0.18) if cuts else 1.0
    values = jax.random.normal(stream_key, shape, jnp.float32) * scale * level
    return jnp.minimum(jnp.maximum(values, -limit), limit).astype(kind)


def setup_inputs(seed: int = 0) -> dict:
    splits = jax.random.split(jax.random.key(seed), 15)
    tokens = scatter_about(splits[0], (BATCH, SEQ, D), 1.0, 6.0, ((0, 2), (1, 8)))
    queries = draw_queries(jax.random.fold_in(splits[14], 71), 0)
    kv_weight = scatter_about(splits[2], (D, LAT + ROPE), D ** -0.5, 0.125, ((0, 2),))
    kv_gain = jnp.clip(1.0 + 0.1 * jax.random.normal(splits[3], (LAT,), jnp.float32), 0.5, 1.5).astype(jnp.bfloat16)
    uv_weight = scatter_about(splits[4], (HEADS, LAT, VH), (LAT // 8) ** -0.5, 0.75, ((0, 2),))
    out_weight = scatter_about(splits[5], (HEADS * VH, D), VH ** -0.5, 0.5, ((0, 2),))
    post_gain = jnp.clip(1.0 + 0.1 * jax.random.normal(splits[6], (D,), jnp.float32), 0.5, 1.5).astype(jnp.bfloat16)
    router_weight = scatter_about(splits[7], (D, EXPERTS), D ** -0.5, 0.125)
    expert_ids_keys = jax.random.split(jax.random.fold_in(splits[8], 1), BATCH * SEQ // SEQ_DEV)
    expert_ids_turns = jax.random.permutation(jax.random.fold_in(splits[8], 3), BATCH * SEQ // SEQ_DEV)
    expert_ids = jax.vmap(lambda own, number: assign_block(jax.random.fold_in(splits[8], 2), own, number, SEQ_DEV, EXPERTS, TOPK, CAP, 2))(expert_ids_keys, expert_ids_turns).reshape((BATCH, SEQ, TOPK))
    doc_ids = jax.vmap(lambda own: jnp.searchsorted(jnp.cumsum(ragged_sizes(own, DOCS, SEQ, SEQ // 2, 0)), jnp.arange(SEQ), side="right"))(jax.random.split(splits[9], BATCH)).reshape((BATCH, SEQ)).astype(jnp.int32)
    gate_weight = scatter_about(splits[10], (EXPERTS, D, FFE), D ** -0.5, 0.125, ((0, 8), (2, 2)))
    up_weight = scatter_about(splits[11], (EXPERTS, D, FFE), D ** -0.5, 0.125, ((0, 8), (2, 2)))
    down_weight = scatter_about(splits[12], (EXPERTS, FFE, D), FFE ** -0.5, 0.15625, ((0, 8), (1, 2)))
    cotangent = scatter_about(splits[13], (BATCH, SEQ, D), 1.0, 6.0, ((0, 2), (1, 8)))
    return {"tokens": tokens, "queries": queries, "kv_weight": kv_weight, "kv_gain": kv_gain, "uv_weight": uv_weight, "out_weight": out_weight, "post_gain": post_gain, "router_weight": router_weight, "expert_ids": expert_ids, "doc_ids": doc_ids, "gate_weight": gate_weight, "up_weight": up_weight, "down_weight": down_weight, "cotangent": cotangent}


epsilon = 1e-06

def rms_scale(values, gain):
    return values * lax.rsqrt(lax.optimization_barrier(jnp.mean(values * values, axis=-1, keepdims=True)) + epsilon) * gain

def rotate(rope_part, positions):
    half_width = rope_part.shape[-1] // 2
    frequency = jnp.power(10000.0, -2.0 * jnp.arange(half_width, dtype=jnp.float32) / rope_part.shape[-1])
    angles = positions.astype(jnp.float32)[:, None] * frequency[None, :]
    cosine = jnp.cos(angles)
    sine_part = jnp.sin(angles)
    first_half = rope_part[:, :half_width]
    second = rope_part[:, half_width:]
    return jnp.concatenate([first_half * cosine - second * sine_part, second * cosine + first_half * sine_part], axis=1)

def attend(token_rows, query_rows, doc_rows, kv_weight, kv_gain, uv_weight, out_weight):
    compressed = jnp.dot(token_rows, kv_weight, preferred_element_type=jnp.float32)
    latent = rms_scale(compressed[:, :LAT], kv_gain.astype(jnp.float32)).astype(jnp.bfloat16)
    positions = jnp.arange(SEQ, dtype=jnp.int32)
    rope_key = rotate(compressed[:, LAT:], positions).astype(jnp.bfloat16)
    key_rows = jnp.concatenate([latent, rope_key], axis=1).astype(jnp.float32)
    latent_wide = latent.astype(jnp.float32)
    score_scale = (NOPE + ROPE) ** (-0.5)

    def block(first_row):
        query_block = lax.dynamic_slice_in_dim(query_rows, first_row, SEQ_DEV, 0).astype(jnp.float32)
        query_pos = first_row + jnp.arange(SEQ_DEV, dtype=jnp.int32)
        query_doc = lax.dynamic_slice_in_dim(doc_rows, first_row, SEQ_DEV, 0)
        scores = jnp.einsum('qhd,kd->qhk', query_block, key_rows) * score_scale
        allowed = (positions[None, :] <= query_pos[:, None]) & (doc_rows[None, :] == query_doc[:, None])
        allowed = allowed[:, None, :]
        score_peak = lax.optimization_barrier(jnp.max(jnp.where(allowed, scores, -1e+30), axis=-1, keepdims=True))
        weights = jnp.exp(jnp.where(allowed, scores - score_peak, -1e+30))
        weight_total = lax.optimization_barrier(jnp.sum(weights, axis=-1, keepdims=True))
        rounded = lax.optimization_barrier(weights.astype(jnp.bfloat16))
        mixed_latent = jnp.einsum('qhk,kl->qhl', rounded.astype(jnp.float32), latent_wide) / weight_total
        return mixed_latent.astype(jnp.bfloat16)
    starts = jnp.arange(SEQ // SEQ_DEV, dtype=jnp.int32) * SEQ_DEV
    mixed_latent = lax.map(block, starts).reshape(SEQ, HEADS, LAT)
    mixed_latent = lax.optimization_barrier(mixed_latent)
    head_values = jnp.einsum('qhl,hlv->qhv', mixed_latent.astype(jnp.float32), uv_weight.astype(jnp.float32))
    head_values = head_values.astype(jnp.bfloat16).reshape(SEQ, HEADS * VH)
    return jnp.dot(head_values, out_weight, preferred_element_type=jnp.float32)

def reference(tokens, queries, kv_weight, kv_gain, uv_weight, out_weight, post_gain, router_weight, expert_ids, doc_ids, gate_weight, up_weight, down_weight, cotangent):
    attention = jnp.stack([attend(tokens[batch_row], queries[batch_row], doc_ids[batch_row], kv_weight, kv_gain, uv_weight, out_weight) for batch_row in range(BATCH)])
    hidden = (tokens.astype(jnp.float32) + attention).astype(jnp.bfloat16)
    normed = rms_scale(hidden.astype(jnp.float32), post_gain.astype(jnp.float32)).astype(jnp.bfloat16)
    flat_rows = normed.reshape(-1, D)
    logits = jnp.dot(flat_rows, router_weight, preferred_element_type=jnp.float32)
    router_probs = jax.nn.softmax(logits, axis=-1)
    flat_ids = expert_ids.reshape(-1, TOPK).astype(jnp.int32)
    chosen = jnp.take_along_axis(router_probs, flat_ids, axis=1)
    chosen_sum = lax.optimization_barrier(jnp.sum(chosen, axis=1, keepdims=True))
    route_w = chosen / chosen_sum
    route_wb = route_w.astype(jnp.bfloat16)
    blocks = BATCH * N_CTX
    block_ids = flat_ids.reshape(blocks, SEQ_DEV * TOPK)
    onehot = (block_ids[:, :, None] == jnp.arange(EXPERTS, dtype=jnp.int32)[None, None, :]).astype(jnp.int32)
    slot_rank = lax.optimization_barrier(jnp.sum((jnp.cumsum(onehot, axis=1) - onehot) * onehot, axis=2))
    slot_index = (block_ids * CAP + slot_rank).reshape(blocks, SEQ_DEV, TOPK)
    block_axis = jnp.arange(blocks, dtype=jnp.int32)[:, None, None]
    row_copies = jnp.broadcast_to(flat_rows.reshape(blocks, SEQ_DEV, 1, D), (blocks, SEQ_DEV, TOPK, D))
    outgoing = jnp.zeros((blocks, EXPERTS * CAP, D), jnp.bfloat16).at[block_axis, slot_index].set(row_copies)
    cot_rows = cotangent.reshape(blocks, SEQ_DEV, 1, D).astype(jnp.float32)
    weighted_cot = (route_wb.astype(jnp.float32).reshape(blocks, SEQ_DEV, TOPK, 1) * cot_rows).astype(jnp.bfloat16)
    slot_cot = jnp.zeros((blocks, EXPERTS * CAP, D), jnp.bfloat16).at[block_axis, slot_index].set(weighted_cot)
    expert_inputs = outgoing.reshape(blocks, EXPERTS, CAP, D).transpose(1, 0, 2, 3)
    expert_cots = slot_cot.reshape(blocks, EXPERTS, CAP, D).transpose(1, 0, 2, 3)
    slice_width = FFE // N_EXP

    def expert(operands):
        inputs, cots, gate_one, up_one, down_one = operands
        input_rows = inputs.reshape(-1, D)
        gate_pre = jnp.dot(input_rows, gate_one, preferred_element_type=jnp.float32)
        up_pre = jnp.dot(input_rows, up_one, preferred_element_type=jnp.float32)
        activated = lax.optimization_barrier((jax.nn.silu(gate_pre) * up_pre).astype(jnp.bfloat16))
        parts = jnp.einsum('rjf,jfd->jrd', activated.astype(jnp.float32).reshape(-1, N_EXP, slice_width), down_one.astype(jnp.float32).reshape(N_EXP, slice_width, D))
        parts = lax.optimization_barrier(parts.astype(jnp.bfloat16))
        expert_out = lax.optimization_barrier(jnp.sum(parts.astype(jnp.float32), axis=0))
        cot_slots = cots.reshape(-1, D)
        down_grad = jnp.dot(activated.T, cot_slots, preferred_element_type=jnp.float32)
        dact = jnp.dot(cot_slots, down_one.T, preferred_element_type=jnp.float32)
        sigmoid_gate = jax.nn.sigmoid(gate_pre)
        dgate = (dact * up_pre * sigmoid_gate * (1.0 + gate_pre * (1.0 - sigmoid_gate))).astype(jnp.bfloat16)
        dup = (dact * gate_pre * sigmoid_gate).astype(jnp.bfloat16)
        gate_grad = jnp.dot(input_rows.T, dgate, preferred_element_type=jnp.float32)
        up_grad = jnp.dot(input_rows.T, dup, preferred_element_type=jnp.float32)
        return (expert_out.reshape(blocks, CAP, D), gate_grad.astype(jnp.bfloat16), up_grad.astype(jnp.bfloat16), down_grad.astype(jnp.bfloat16))
    expert_out, gate_grad, up_grad, down_grad = lax.map(expert, (expert_inputs, expert_cots, gate_weight, up_weight, down_weight))
    block_out = expert_out.transpose(1, 0, 2, 3).reshape(blocks, EXPERTS * CAP, D)
    picked = block_out[block_axis, slot_index].reshape(-1, TOPK, D)
    moe = lax.optimization_barrier(jnp.sum(route_wb.astype(jnp.float32)[:, :, None] * picked, axis=1))
    layer_out = (hidden.astype(jnp.float32) + moe.reshape(BATCH, SEQ, D)).astype(jnp.bfloat16)
    cot_flat = cotangent.reshape(-1, D).astype(jnp.float32)
    dweight = lax.optimization_barrier(jnp.sum(cot_flat[:, None, :] * picked, axis=2))
    mean_term = lax.optimization_barrier(jnp.sum(dweight * route_w, axis=1, keepdims=True))
    dchosen = (dweight - mean_term) / chosen_sum
    id_hits = (flat_ids[:, :, None] == jnp.arange(EXPERTS, dtype=jnp.int32)[None, None, :]).astype(jnp.float32)
    dprobs = lax.optimization_barrier(jnp.sum(id_hits * dchosen[:, :, None], axis=1))
    dlogits = router_probs * (dprobs - lax.optimization_barrier(jnp.sum(router_probs * dprobs, axis=1, keepdims=True)))
    router_grad = jnp.dot(flat_rows.astype(jnp.float32).T, dlogits, precision=lax.Precision.HIGHEST)
    return (layer_out, router_grad, gate_grad, up_grad, down_grad)
```

```python
import jax
import jax.numpy as jnp
from jax import lax
from jax.sharding import PartitionSpec as P

ROPE = 64
NOPE = 128


epsilon = 1e-06


def rms_scale(values, gain):
    return values * lax.rsqrt(jnp.mean(values * values, axis=-1, keepdims=True) + epsilon) * gain


def rotate(rope_part, positions):
    half_width = rope_part.shape[-1] // 2
    frequency = jnp.power(
        10000.0, -2.0 * jnp.arange(half_width, dtype=jnp.float32) / rope_part.shape[-1]
    )
    angles = positions.astype(jnp.float32)[:, None] * frequency[None, :]
    cosine = jnp.cos(angles)
    sine_part = jnp.sin(angles)
    first_half = rope_part[:, :half_width]
    second = rope_part[:, half_width:]
    return jnp.concatenate(
        [first_half * cosine - second * sine_part, second * cosine + first_half * sine_part], axis=1
    )


def from_peer(values, axis):
    return lax.ppermute(values, axis, [(0, 1), (1, 0)])


def sum_over(values, axis):
    if lax.axis_size(axis) == 2:
        return values + from_peer(values, axis)
    return lax.psum(values, axis)


def scatter_rows(values, axis):
    if lax.axis_size(axis) > 2:
        return lax.psum_scatter(values, axis, scatter_dimension=0, tiled=True)
    share = values.shape[0] // 2
    at = lax.axis_index(axis)
    own = lax.dynamic_slice_in_dim(values, at * share, share, 0)
    sent = lax.dynamic_slice_in_dim(values, (1 - at) * share, share, 0)
    return own + from_peer(sent, axis)


def split_parts(values):
    high = lax.reduce_precision(values, 8, 7)
    rest = values - high
    middle = lax.reduce_precision(rest, 8, 7)
    return jnp.concatenate([high, middle, rest - middle], axis=1).astype(jnp.bfloat16)


def local(
    tokens,
    queries,
    kv_weight,
    kv_gain,
    uv_weight,
    out_weight,
    post_gain,
    router_weight,
    expert_ids,
    doc_ids,
    gate_weight,
    up_weight,
    down_weight,
    cotangent,
):
    bf16, f32 = jnp.bfloat16, jnp.float32
    local_rows = tokens[0]
    seq_rows = local_rows.shape[0]
    half_rows = seq_rows // lax.axis_size("exp")
    model_width = local_rows.shape[1]
    half_width = model_width // 2
    latent_width = kv_gain.shape[0]
    row_share = kv_weight.shape[0]
    dp_at, ctx_at, exp_at = (lax.axis_index(name) for name in ("dp", "ctx", "exp"))
    ctx_count = lax.axis_size("ctx")

    cot_all = lax.all_gather(cotangent[0], "ctx", axis=0, tiled=True)

    columns = lax.dynamic_slice_in_dim(local_rows, exp_at * row_share, row_share, 1)
    compressed = jnp.dot(columns, kv_weight, preferred_element_type=f32)
    compressed = sum_over(compressed, "exp")
    positions = ctx_at * seq_rows + jnp.arange(seq_rows, dtype=jnp.int32)
    latent = rms_scale(compressed[:, :latent_width], kv_gain.astype(f32)).astype(bf16)
    rope_key = rotate(compressed[:, latent_width:], positions).astype(bf16)
    key_width = latent_width + rope_key.shape[1]
    key_rows = jnp.concatenate(
        [latent, rope_key, expert_ids[0].astype(bf16), doc_ids[0][:, None].astype(bf16)], axis=1
    )
    gathered = lax.all_gather(key_rows, "ctx", axis=0, tiled=True)
    all_keys = gathered[:, :key_width]
    ids_all = gathered[:, key_width:-1].astype(jnp.int32)
    all_docs = gathered[:, -1].astype(jnp.int32)

    experts_all = router_weight.shape[1]
    top_count = ids_all.shape[1]
    held = experts_all // ctx_count
    capacity = (4 * seq_rows * top_count + 3 * experts_all - 1) // (3 * experts_all)
    member = jnp.any(
        ids_all[:, :, None] == jnp.arange(experts_all, dtype=jnp.int32)[None, None, :], axis=1
    )
    member_f = member.astype(f32)
    member_own = lax.dynamic_slice_in_dim(member_f, ctx_at * held, held, 1).reshape(
        ctx_count, seq_rows, held
    )
    before = jnp.tril(jnp.ones((seq_rows, seq_rows), bf16), -1)
    rank = jnp.einsum(
        "ut,stj->sju", before, member_own.astype(bf16), preferred_element_type=f32
    ).astype(jnp.int32)
    hits = (rank[:, :, None, :] == jnp.arange(capacity, dtype=jnp.int32)[None, None, :, None]) & (
        jnp.moveaxis(member_own, 1, 2)[:, :, None, :] > 0
    )
    dispatch = hits.astype(bf16).reshape(ctx_count, held * capacity, seq_rows)

    def to_slots(rows):
        return jnp.einsum(
            "sct,std->scd",
            dispatch,
            rows.reshape(ctx_count, seq_rows, model_width),
            preferred_element_type=f32,
        ).astype(bf16).reshape(ctx_count, held, capacity, model_width)

    def own_half(rows):
        return lax.dynamic_slice_in_dim(rows, dp_at * half_width, half_width, rows.ndim - 1)

    def peer_half(rows):
        other = lax.dynamic_slice_in_dim(rows, (1 - dp_at) * half_width, half_width, rows.ndim - 1)
        return from_peer(other, "dp")

    allowed = (jnp.arange(all_keys.shape[0], dtype=jnp.int32)[None, :] <= positions[:, None]) & (
        all_docs[None, :] == doc_ids[0][:, None]
    )
    allowed = allowed[:, None, :]
    score_scale = (NOPE + ROPE) ** (-0.5)
    scores = (
        jnp.einsum("qhd,kd->qhk", queries[0], all_keys, preferred_element_type=f32) * score_scale
    )
    score_peak = jnp.max(jnp.where(allowed, scores, -1e30), axis=-1, keepdims=True)
    weights = jnp.exp(jnp.where(allowed, scores - score_peak, -1e30))
    weight_total = jnp.sum(weights, axis=-1, keepdims=True)
    mixed_latent = (
        jnp.einsum(
            "qhk,kl->qhl",
            weights.astype(bf16),
            all_keys[:, :latent_width],
            preferred_element_type=f32,
        )
        / weight_total
    ).astype(bf16)
    head_values = (
        jnp.einsum("qhl,hlv->qhv", mixed_latent, uv_weight, preferred_element_type=f32)
        .astype(bf16)
        .reshape(seq_rows, -1)
    )
    head_part = jnp.dot(head_values, out_weight, preferred_element_type=f32)
    attention = scatter_rows(head_part, "exp")
    token_rows = lax.dynamic_slice_in_dim(local_rows, exp_at * half_rows, half_rows, 0)
    hidden = (token_rows.astype(f32) + attention).astype(bf16)
    normed = rms_scale(hidden.astype(f32), post_gain.astype(f32)).astype(bf16)
    normed_all = lax.all_gather(normed, ("ctx", "exp"), axis=0, tiled=True)

    cot_slots = to_slots(cot_all)
    cot_peer = peer_half(cot_slots)
    dact_raw = jnp.einsum("sjcd,jfd->sjcf", cot_slots, down_weight, preferred_element_type=f32)

    arrived = to_slots(normed_all)
    arrived_peer = peer_half(arrived)
    logits = jnp.dot(normed_all, router_weight, preferred_element_type=f32)
    router_probs = jax.nn.softmax(logits, axis=-1)
    chosen = router_probs * member_f
    chosen_sum = jnp.sum(chosen, axis=1, keepdims=True)
    route_w = chosen / chosen_sum
    route_own = lax.dynamic_slice_in_dim(route_w, ctx_at * held, held, 1).reshape(
        ctx_count, seq_rows, held
    )
    route_own = lax.reduce_precision(jnp.moveaxis(route_own, 1, 2), 8, 7)
    slot_w = jnp.sum(jnp.where(hits, route_own[:, :, None, :], 0.0), axis=3)
    combine = jnp.where(hits, route_own[:, :, None, :], 0.0).astype(bf16).reshape(
        ctx_count, held * capacity, seq_rows
    )

    gate_pre = jnp.einsum("sjcd,jdf->sjcf", arrived, gate_weight, preferred_element_type=f32)
    up_pre = jnp.einsum("sjcd,jdf->sjcf", arrived, up_weight, preferred_element_type=f32)
    sigmoid_gate = jax.nn.sigmoid(gate_pre)
    activated = (gate_pre * sigmoid_gate * up_pre).astype(bf16)
    expert_part = jnp.einsum(
        "sjcf,jfd->sjcd", activated, down_weight, preferred_element_type=f32
    ).astype(bf16)
    moe_part = jnp.einsum(
        "sct,scd->std",
        combine,
        expert_part.reshape(ctx_count, held * capacity, model_width),
        preferred_element_type=f32,
    ).astype(bf16)
    moe = lax.psum_scatter(
        moe_part.reshape(-1, model_width), ("ctx", "exp"), scatter_dimension=0, tiled=True
    )

    weighted = (activated.astype(f32) * slot_w[..., None]).astype(bf16)
    dact = dact_raw * slot_w[..., None]
    dgate = (dact * up_pre * sigmoid_gate * (1.0 + gate_pre * (1.0 - sigmoid_gate))).astype(bf16)
    dup = (dact * gate_pre * sigmoid_gate).astype(bf16)
    weighted_peer, dgate_peer, dup_peer = (
        from_peer(weighted, "dp"),
        from_peer(dgate, "dp"),
        from_peer(dup, "dp"),
    )

    dweight_slot = jnp.sum(activated.astype(f32) * dact_raw, axis=-1)
    dweight_part = jnp.sum(jnp.where(hits, dweight_slot[..., None], 0.0), axis=2)
    dweight_part = jnp.moveaxis(dweight_part, 1, 2).reshape(-1, held)
    dweight_each = lax.all_gather(dweight_part.T, ("ctx", "exp"), axis=0, tiled=False)
    dweight_each = dweight_each.reshape(ctx_count, -1, held, dweight_part.shape[0])
    dweight = jnp.sum(dweight_each, axis=1).reshape(experts_all, -1).T
    mean_term = jnp.sum(dweight * route_w, axis=1, keepdims=True)
    dprobs = member_f * (dweight - mean_term) / chosen_sum
    dlogits = router_probs * (dprobs - jnp.sum(router_probs * dprobs, axis=1, keepdims=True))
    router_parts = jnp.einsum(
        "td,te->de", normed_all, split_parts(dlogits), preferred_element_type=f32
    )
    router_term = jnp.sum(router_parts.reshape(model_width, 3, experts_all), axis=1)
    router_grad = router_term + from_peer(router_term, "dp")

    def summed(form, own, own_other, peer, peer_other):
        first = jnp.einsum(form, own, own_other, preferred_element_type=f32)
        second = jnp.einsum(form, peer, peer_other, preferred_element_type=f32)
        return (first + second).astype(bf16)

    arrived_own = own_half(arrived)
    gate_out = summed("sjcd,sjcf->jdf", arrived_own, dgate, arrived_peer, dgate_peer)
    up_out = summed("sjcd,sjcf->jdf", arrived_own, dup, arrived_peer, dup_peer)
    down_out = summed("sjcf,sjcd->jfd", weighted, own_half(cot_slots), weighted_peer, cot_peer)

    layer_half = (hidden.astype(f32) + moe.astype(f32)).astype(bf16)
    layer_out = lax.all_gather(layer_half, "exp", axis=0, tiled=True)
    return (layer_out[None], router_grad, gate_out, up_out, down_out)


def solution(mesh):
    placed = (
        P("dp", "ctx", None),
        P("dp", "ctx", "exp", None),
        P("exp", None),
        P(),
        P("exp", None, None),
        P("exp", None),
        P(),
        P(),
        P("dp", "ctx", None),
        P("dp", "ctx"),
        P("ctx", None, "exp"),
        P("ctx", None, "exp"),
        P("ctx", "exp", None),
        P("dp", "ctx", None),
    )
    return jax.shard_map(
        local,
        mesh=mesh,
        in_specs=placed,
        out_specs=(
            P("dp", "ctx", None),
            P(),
            P("ctx", "dp", "exp"),
            P("ctx", "dp", "exp"),
            P("ctx", "exp", "dp"),
        ),
        check_vma=False,
    )
```

```python
import jax
import jax.numpy as jnp
from jax import lax
from jax.sharding import PartitionSpec as P

ROPE = 64
NOPE = 128


epsilon = 1e-06


def rms_scale(values, gain):
    return values * lax.rsqrt(jnp.mean(values * values, axis=-1, keepdims=True) + epsilon) * gain


def rotate(rope_part, positions):
    half_width = rope_part.shape[-1] // 2
    frequency = jnp.power(
        10000.0, -2.0 * jnp.arange(half_width, dtype=jnp.float32) / rope_part.shape[-1]
    )
    angles = positions.astype(jnp.float32)[:, None] * frequency[None, :]
    cosine = jnp.cos(angles)
    sine_part = jnp.sin(angles)
    first_half = rope_part[:, :half_width]
    second = rope_part[:, half_width:]
    return jnp.concatenate(
        [first_half * cosine - second * sine_part, second * cosine + first_half * sine_part], axis=1
    )


def from_peer(values, axis):
    return lax.ppermute(values, axis, [(0, 1), (1, 0)])


def sum_over(values, axis):
    if lax.axis_size(axis) == 2:
        return values + from_peer(values, axis)
    return lax.psum(values, axis)


def scatter_rows(values, axis):
    if lax.axis_size(axis) > 2:
        return lax.psum_scatter(values, axis, scatter_dimension=0, tiled=True)
    share = values.shape[0] // 2
    at = lax.axis_index(axis)
    own = lax.dynamic_slice_in_dim(values, at * share, share, 0)
    sent = lax.dynamic_slice_in_dim(values, (1 - at) * share, share, 0)
    return own + from_peer(sent, axis)


def gather_pairs(values, axis):
    pairs = lax.axis_size(axis) // 2
    at = lax.axis_index(axis)
    outer, inner = at // 2, lax.rem(at, 2)
    swap = [(i, i ^ 1) for i in range(2 * pairs)]
    blocks, owners = [], []
    for step in range(pairs):
        shift = [(i, (i + 2 * step) % (2 * pairs)) for i in range(2 * pairs)]
        block = values if step == 0 else lax.ppermute(values, axis, shift)
        source = lax.rem(outer + pairs - step, pairs) * 2
        blocks += [block, lax.ppermute(block, axis, swap)]
        owners += [source + inner, source + 1 - inner]
    return blocks, owners


def in_order(blocks, owners):
    whole = jnp.zeros((len(blocks),) + blocks[0].shape, blocks[0].dtype)
    for block, owner in zip(blocks, owners):
        whole = lax.dynamic_update_index_in_dim(whole, block, owner, 0)
    return whole


def split_parts(values):
    high = lax.reduce_precision(values, 8, 7)
    rest = values - high
    middle = lax.reduce_precision(rest, 8, 7)
    return jnp.concatenate([high, middle, rest - middle], axis=1).astype(jnp.bfloat16)


def local(
    tokens,
    queries,
    kv_weight,
    kv_gain,
    uv_weight,
    out_weight,
    post_gain,
    router_weight,
    expert_ids,
    doc_ids,
    gate_weight,
    up_weight,
    down_weight,
    cotangent,
):
    bf16, f32 = jnp.bfloat16, jnp.float32
    local_rows = tokens[0]
    seq_rows = local_rows.shape[0]
    half_rows = seq_rows // lax.axis_size("exp")
    model_width = local_rows.shape[1]
    half_width = model_width // 2
    latent_width = kv_gain.shape[0]
    row_share = kv_weight.shape[0]
    dp_at, ctx_at, exp_at = (lax.axis_index(name) for name in ("dp", "ctx", "exp"))
    ctx_count = lax.axis_size("ctx")

    cot_all = lax.all_gather(cotangent[0], "ctx", axis=0, tiled=True)

    columns = lax.dynamic_slice_in_dim(local_rows, exp_at * row_share, row_share, 1)
    compressed = jnp.dot(columns, kv_weight, preferred_element_type=f32)
    compressed = sum_over(compressed, "exp")
    positions = ctx_at * seq_rows + jnp.arange(seq_rows, dtype=jnp.int32)
    latent = rms_scale(compressed[:, :latent_width], kv_gain.astype(f32)).astype(bf16)
    rope_key = rotate(compressed[:, latent_width:], positions).astype(bf16)
    key_width = latent_width + rope_key.shape[1]
    key_rows = jnp.concatenate(
        [latent, rope_key, expert_ids[0].astype(bf16), doc_ids[0][:, None].astype(bf16)], axis=1
    )
    key_blocks, owners = gather_pairs(key_rows, "ctx")
    all_keys = jnp.concatenate([block[:, :key_width] for block in key_blocks], axis=0)
    all_docs = jnp.concatenate([block[:, -1] for block in key_blocks], axis=0).astype(jnp.int32)
    key_positions = jnp.concatenate(
        [owner * seq_rows + jnp.arange(seq_rows, dtype=jnp.int32) for owner in owners]
    )
    ids_all = in_order([block[:, key_width:-1] for block in key_blocks], owners)
    ids_all = ids_all.reshape(-1, ids_all.shape[-1]).astype(jnp.int32)

    experts_all = router_weight.shape[1]
    top_count = ids_all.shape[1]
    held = experts_all // ctx_count
    capacity = (4 * seq_rows * top_count + 3 * experts_all - 1) // (3 * experts_all)
    member = jnp.any(
        ids_all[:, :, None] == jnp.arange(experts_all, dtype=jnp.int32)[None, None, :], axis=1
    )
    member_f = member.astype(f32)
    member_own = lax.dynamic_slice_in_dim(member_f, ctx_at * held, held, 1).reshape(
        ctx_count, seq_rows, held
    )
    before = jnp.tril(jnp.ones((seq_rows, seq_rows), bf16), -1)
    rank = jnp.einsum(
        "ut,stj->sju", before, member_own.astype(bf16), preferred_element_type=f32
    ).astype(jnp.int32)
    hits = (rank[:, :, None, :] == jnp.arange(capacity, dtype=jnp.int32)[None, None, :, None]) & (
        jnp.moveaxis(member_own, 1, 2)[:, :, None, :] > 0
    )
    dispatch = hits.astype(bf16).reshape(ctx_count, held * capacity, seq_rows)

    def to_slots(rows):
        return jnp.einsum(
            "sct,std->scd",
            dispatch,
            rows.reshape(ctx_count, seq_rows, model_width),
            preferred_element_type=f32,
        ).astype(bf16).reshape(ctx_count, held, capacity, model_width)

    def own_half(rows):
        return lax.dynamic_slice_in_dim(rows, dp_at * half_width, half_width, rows.ndim - 1)

    def peer_half(rows):
        other = lax.dynamic_slice_in_dim(rows, (1 - dp_at) * half_width, half_width, rows.ndim - 1)
        return from_peer(other, "dp")

    allowed = (key_positions[None, :] <= positions[:, None]) & (
        all_docs[None, :] == doc_ids[0][:, None]
    )
    allowed = allowed[:, None, :]
    score_scale = (NOPE + ROPE) ** (-0.5)
    scores = (
        jnp.einsum("qhd,kd->qhk", queries[0], all_keys, preferred_element_type=f32) * score_scale
    )
    score_peak = jnp.max(jnp.where(allowed, scores, -1e30), axis=-1, keepdims=True)
    weights = jnp.exp(jnp.where(allowed, scores - score_peak, -1e30))
    weight_total = jnp.sum(weights, axis=-1, keepdims=True)
    mixed_latent = (
        jnp.einsum(
            "qhk,kl->qhl",
            weights.astype(bf16),
            all_keys[:, :latent_width],
            preferred_element_type=f32,
        )
        / weight_total
    ).astype(bf16)
    head_values = (
        jnp.einsum("qhl,hlv->qhv", mixed_latent, uv_weight, preferred_element_type=f32)
        .astype(bf16)
        .reshape(seq_rows, -1)
    )
    head_part = jnp.dot(head_values, out_weight, preferred_element_type=f32)
    attention = scatter_rows(head_part, "exp")
    token_rows = lax.dynamic_slice_in_dim(local_rows, exp_at * half_rows, half_rows, 0)
    hidden = (token_rows.astype(f32) + attention).astype(bf16)
    normed = rms_scale(hidden.astype(f32), post_gain.astype(f32)).astype(bf16)
    normed_all = lax.all_gather(normed, ("ctx", "exp"), axis=0, tiled=True)

    cot_slots = to_slots(cot_all)
    cot_peer = peer_half(cot_slots)
    dact_raw = jnp.einsum("sjcd,jfd->sjcf", cot_slots, down_weight, preferred_element_type=f32)

    arrived = to_slots(normed_all)
    arrived_peer = peer_half(arrived)
    logits = jnp.dot(normed_all, router_weight, preferred_element_type=f32)
    router_probs = jax.nn.softmax(logits, axis=-1)
    chosen = router_probs * member_f
    chosen_sum = jnp.sum(chosen, axis=1, keepdims=True)
    route_w = chosen / chosen_sum
    route_own = lax.dynamic_slice_in_dim(route_w, ctx_at * held, held, 1).reshape(
        ctx_count, seq_rows, held
    )
    route_own = lax.reduce_precision(jnp.moveaxis(route_own, 1, 2), 8, 7)
    slot_w = jnp.sum(jnp.where(hits, route_own[:, :, None, :], 0.0), axis=3)
    combine = jnp.where(hits, route_own[:, :, None, :], 0.0).astype(bf16).reshape(
        ctx_count, held * capacity, seq_rows
    )

    gate_pre = jnp.einsum("sjcd,jdf->sjcf", arrived, gate_weight, preferred_element_type=f32)
    up_pre = jnp.einsum("sjcd,jdf->sjcf", arrived, up_weight, preferred_element_type=f32)
    sigmoid_gate = jax.nn.sigmoid(gate_pre)
    activated = (gate_pre * sigmoid_gate * up_pre).astype(bf16)
    expert_part = jnp.einsum(
        "sjcf,jfd->sjcd", activated, down_weight, preferred_element_type=f32
    ).astype(bf16)
    moe_part = jnp.einsum(
        "sct,scd->std",
        combine,
        expert_part.reshape(ctx_count, held * capacity, model_width),
        preferred_element_type=f32,
    ).astype(bf16)
    moe = lax.psum_scatter(
        moe_part.reshape(-1, model_width), ("ctx", "exp"), scatter_dimension=0, tiled=True
    )

    weighted = (activated.astype(f32) * slot_w[..., None]).astype(bf16)
    dact = dact_raw * slot_w[..., None]
    dgate = (dact * up_pre * sigmoid_gate * (1.0 + gate_pre * (1.0 - sigmoid_gate))).astype(bf16)
    dup = (dact * gate_pre * sigmoid_gate).astype(bf16)
    weighted_peer, dgate_peer, dup_peer = (
        from_peer(weighted, "dp"),
        from_peer(dgate, "dp"),
        from_peer(dup, "dp"),
    )

    dweight_slot = jnp.sum(activated.astype(f32) * dact_raw, axis=-1)
    dweight_part = jnp.sum(jnp.where(hits, dweight_slot[..., None], 0.0), axis=2)
    dweight_part = jnp.moveaxis(dweight_part, 1, 0).reshape(held, -1)
    dweight = in_order(*gather_pairs(sum_over(dweight_part, "exp"), "ctx"))
    dweight = dweight.reshape(experts_all, -1).T
    mean_term = jnp.sum(dweight * route_w, axis=1, keepdims=True)
    dprobs = member_f * (dweight - mean_term) / chosen_sum
    dlogits = router_probs * (dprobs - jnp.sum(router_probs * dprobs, axis=1, keepdims=True))
    router_parts = jnp.einsum(
        "td,te->de", normed_all, split_parts(dlogits), preferred_element_type=f32
    )
    router_term = jnp.sum(router_parts.reshape(model_width, 3, experts_all), axis=1)
    router_grad = router_term + from_peer(router_term, "dp")

    def summed(form, own, own_other, peer, peer_other):
        first = jnp.einsum(form, own, own_other, preferred_element_type=f32)
        second = jnp.einsum(form, peer, peer_other, preferred_element_type=f32)
        return (first + second).astype(bf16)

    arrived_own = own_half(arrived)
    gate_out = summed("sjcd,sjcf->jdf", arrived_own, dgate, arrived_peer, dgate_peer)
    up_out = summed("sjcd,sjcf->jdf", arrived_own, dup, arrived_peer, dup_peer)
    down_out = summed("sjcf,sjcd->jfd", weighted, own_half(cot_slots), weighted_peer, cot_peer)

    layer_half = (hidden.astype(f32) + moe.astype(f32)).astype(bf16)
    if lax.axis_size("exp") == 2:
        other_half = from_peer(layer_half, "exp")
        layer_out = jnp.concatenate(
            [
                jnp.where(exp_at == 0, layer_half, other_half),
                jnp.where(exp_at == 0, other_half, layer_half),
            ],
            axis=0,
        )
    else:
        layer_out = lax.all_gather(layer_half, "exp", axis=0, tiled=True)
    return (layer_out[None], router_grad, gate_out, up_out, down_out)


def solution(mesh):
    placed = (
        P("dp", "ctx", None),
        P("dp", "ctx", "exp", None),
        P("exp", None),
        P(),
        P("exp", None, None),
        P("exp", None),
        P(),
        P(),
        P("dp", "ctx", None),
        P("dp", "ctx"),
        P("ctx", None, "exp"),
        P("ctx", None, "exp"),
        P("ctx", "exp", None),
        P("dp", "ctx", None),
    )
    return jax.shard_map(
        local,
        mesh=mesh,
        in_specs=placed,
        out_specs=(
            P("dp", "ctx", None),
            P(),
            P("ctx", "dp", "exp"),
            P("ctx", "dp", "exp"),
            P("ctx", "exp", "dp"),
        ),
        check_vma=False,
    )
```

```python
import jax
import jax.numpy as jnp
from jax import lax
from jax.experimental import pallas as pl
from jax.experimental.pallas import tpu as pltpu
from jax.sharding import PartitionSpec as P

ROPE = 64
NOPE = 128


epsilon = 1e-06


def rms_scale(values, gain):
    return values * lax.rsqrt(jnp.mean(values * values, axis=-1, keepdims=True) + epsilon) * gain


def rotate(rope_part, positions):
    half_width = rope_part.shape[-1] // 2
    frequency = jnp.power(
        10000.0, -2.0 * jnp.arange(half_width, dtype=jnp.float32) / rope_part.shape[-1]
    )
    angles = positions.astype(jnp.float32)[:, None] * frequency[None, :]
    cosine = jnp.cos(angles)
    sine_part = jnp.sin(angles)
    first_half = rope_part[:, :half_width]
    second = rope_part[:, half_width:]
    return jnp.concatenate(
        [first_half * cosine - second * sine_part, second * cosine + first_half * sine_part], axis=1
    )


def from_peer(values, axis):
    return lax.ppermute(values, axis, [(0, 1), (1, 0)])


def sum_over(values, axis):
    if lax.axis_size(axis) == 2:
        return values + from_peer(values, axis)
    return lax.psum(values, axis)


def scatter_rows(values, axis):
    if lax.axis_size(axis) > 2:
        return lax.psum_scatter(values, axis, scatter_dimension=0, tiled=True)
    share = values.shape[0] // 2
    at = lax.axis_index(axis)
    own = lax.dynamic_slice_in_dim(values, at * share, share, 0)
    sent = lax.dynamic_slice_in_dim(values, (1 - at) * share, share, 0)
    return own + from_peer(sent, axis)


def gather_pairs(values, axis):
    pairs = lax.axis_size(axis) // 2
    at = lax.axis_index(axis)
    outer, inner = at // 2, lax.rem(at, 2)
    swap = [(i, i ^ 1) for i in range(2 * pairs)]
    blocks, owners = [], []
    for step in range(pairs):
        shift = [(i, (i + 2 * step) % (2 * pairs)) for i in range(2 * pairs)]
        block = values if step == 0 else lax.ppermute(values, axis, shift)
        source = lax.rem(outer + pairs - step, pairs) * 2
        blocks += [block, lax.ppermute(block, axis, swap)]
        owners += [source + inner, source + 1 - inner]
    return blocks, owners


def in_order(blocks, owners):
    whole = jnp.zeros((len(blocks),) + blocks[0].shape, blocks[0].dtype)
    for block, owner in zip(blocks, owners):
        whole = lax.dynamic_update_index_in_dim(whole, block, owner, 0)
    return whole


def gather_kernel(block_ref, out_ref, own_sem, send_sems, recv_sems):
    ctx, exp = lax.axis_index("ctx"), lax.axis_index("exp")
    pairs = lax.axis_size("ctx") // 2
    outer, inner = ctx // 2, lax.rem(ctx, 2)
    rows, width = block_ref.shape
    half = width // 2
    far = [None] + [{"ctx": lax.rem(outer + k, pairs) * 2 + inner} for k in range(1, pairs)]
    pair, twin = {"ctx": outer * 2 + 1 - inner}, {"exp": 1 - exp}

    barrier = pltpu.get_barrier_semaphore()
    for device in far[1:] + [pair, twin]:
        pl.semaphore_signal(barrier, inc=1, device_id=device, device_id_type=pl.DeviceIdType.MESH)
    pl.semaphore_wait(barrier, pairs + 1)

    def place(at_outer, at_inner, at_exp, part):
        row = pl.multiple_of(((at_outer * 2 + at_inner) * 2 + at_exp) * rows, rows)
        return out_ref.at[pl.ds(row, rows), pl.ds(part * half, half)]

    copies = []

    def send(source, target, device):
        at = len(copies)
        copy = pltpu.make_async_remote_copy(
            src_ref=source,
            dst_ref=target,
            send_sem=send_sems.at[at],
            recv_sem=recv_sems.at[at],
            device_id=device,
            device_id_type=pl.DeviceIdType.MESH,
        )
        copy.start()
        copies.append(copy)
        return copy

    own = [block_ref.at[:, pl.ds(part * half, half)] for part in range(2)]
    along = [
        [send(own[part], place(outer, inner, exp, part), far[k]) for part in range(2)]
        for k in range(1, pairs)
    ]
    own_row = pl.multiple_of((ctx * 2 + exp) * rows, rows)
    own_copy = pltpu.make_async_copy(block_ref, out_ref.at[pl.ds(own_row, rows), :], own_sem)
    own_copy.start()
    first, last = [], []
    for step in range(pairs):
        source = lax.rem(outer + pairs - step, pairs)
        held = own
        if step:
            for copy in along[step - 1]:
                copy.wait_recv()
            held = [place(source, inner, exp, part) for part in range(2)]
        targets = [place(source, inner, exp, part) for part in range(2)]
        first.append((send(held[0], targets[0], pair), send(held[1], targets[1], twin)))
        last += [send(held[0], targets[0], twin), send(held[1], targets[1], pair)]
    for step in range(pairs):
        source = lax.rem(outer + pairs - step, pairs)
        left, right = first[step]
        left.wait_recv()
        block = place(source, 1 - inner, exp, 0)
        last.append(send(block, block, twin))
        right.wait_recv()
        block = place(source, inner, 1 - exp, 1)
        last.append(send(block, block, pair))
    for copy in last:
        copy.wait_recv()
    for copy in copies:
        copy.wait_send()
    own_copy.wait()


def gather_rows(block):
    pairs = lax.axis_size("ctx") // 2
    if lax.axis_size("exp") != 2:
        return lax.all_gather(block, ("ctx", "exp"), axis=0, tiled=True)
    count = 8 * pairs - 2
    return pl.pallas_call(
        gather_kernel,
        out_shape=jax.ShapeDtypeStruct((4 * pairs * block.shape[0], block.shape[1]), block.dtype),
        in_specs=[pl.BlockSpec(memory_space=pl.ANY)],
        out_specs=pl.BlockSpec(memory_space=pl.ANY),
        scratch_shapes=[
            pltpu.SemaphoreType.DMA,
            pltpu.SemaphoreType.DMA((count,)),
            pltpu.SemaphoreType.DMA((count,)),
        ],
        compiler_params=pltpu.CompilerParams(collective_id=0, has_side_effects=True),
    )(block)


def split_parts(values):
    high = lax.reduce_precision(values, 8, 7)
    rest = values - high
    middle = lax.reduce_precision(rest, 8, 7)
    return jnp.concatenate([high, middle, rest - middle], axis=1).astype(jnp.bfloat16)


def local(
    tokens,
    queries,
    kv_weight,
    kv_gain,
    uv_weight,
    out_weight,
    post_gain,
    router_weight,
    expert_ids,
    doc_ids,
    gate_weight,
    up_weight,
    down_weight,
    cotangent,
):
    bf16, f32 = jnp.bfloat16, jnp.float32
    local_rows = tokens[0]
    seq_rows = local_rows.shape[0]
    half_rows = seq_rows // lax.axis_size("exp")
    model_width = local_rows.shape[1]
    half_width = model_width // 2
    latent_width = kv_gain.shape[0]
    row_share = kv_weight.shape[0]
    dp_at, ctx_at, exp_at = (lax.axis_index(name) for name in ("dp", "ctx", "exp"))
    ctx_count = lax.axis_size("ctx")

    cot_all = lax.all_gather(cotangent[0], "ctx", axis=0, tiled=True)

    columns = lax.dynamic_slice_in_dim(local_rows, exp_at * row_share, row_share, 1)
    compressed = jnp.dot(columns, kv_weight, preferred_element_type=f32)
    compressed = sum_over(compressed, "exp")
    positions = ctx_at * seq_rows + jnp.arange(seq_rows, dtype=jnp.int32)
    latent = rms_scale(compressed[:, :latent_width], kv_gain.astype(f32)).astype(bf16)
    rope_key = rotate(compressed[:, latent_width:], positions).astype(bf16)
    key_width = latent_width + rope_key.shape[1]
    key_rows = jnp.concatenate(
        [latent, rope_key, expert_ids[0].astype(bf16), doc_ids[0][:, None].astype(bf16)], axis=1
    )
    key_blocks, owners = gather_pairs(key_rows, "ctx")
    all_keys = jnp.concatenate([block[:, :key_width] for block in key_blocks], axis=0)
    all_docs = jnp.concatenate([block[:, -1] for block in key_blocks], axis=0).astype(jnp.int32)
    key_positions = jnp.concatenate(
        [owner * seq_rows + jnp.arange(seq_rows, dtype=jnp.int32) for owner in owners]
    )
    ids_all = in_order([block[:, key_width:-1] for block in key_blocks], owners)
    ids_all = ids_all.reshape(-1, ids_all.shape[-1]).astype(jnp.int32)

    experts_all = router_weight.shape[1]
    top_count = ids_all.shape[1]
    held = experts_all // ctx_count
    capacity = (4 * seq_rows * top_count + 3 * experts_all - 1) // (3 * experts_all)
    member = jnp.any(
        ids_all[:, :, None] == jnp.arange(experts_all, dtype=jnp.int32)[None, None, :], axis=1
    )
    member_f = member.astype(f32)
    member_own = lax.dynamic_slice_in_dim(member_f, ctx_at * held, held, 1).reshape(
        ctx_count, seq_rows, held
    )
    before = jnp.tril(jnp.ones((seq_rows, seq_rows), bf16), -1)
    rank = jnp.einsum(
        "ut,stj->sju", before, member_own.astype(bf16), preferred_element_type=f32
    ).astype(jnp.int32)
    hits = (rank[:, :, None, :] == jnp.arange(capacity, dtype=jnp.int32)[None, None, :, None]) & (
        jnp.moveaxis(member_own, 1, 2)[:, :, None, :] > 0
    )
    dispatch = hits.astype(bf16).reshape(ctx_count, held * capacity, seq_rows)

    def to_slots(rows):
        return jnp.einsum(
            "sct,std->scd",
            dispatch,
            rows.reshape(ctx_count, seq_rows, model_width),
            preferred_element_type=f32,
        ).astype(bf16).reshape(ctx_count, held, capacity, model_width)

    def own_half(rows):
        return lax.dynamic_slice_in_dim(rows, dp_at * half_width, half_width, rows.ndim - 1)

    def peer_half(rows):
        other = lax.dynamic_slice_in_dim(rows, (1 - dp_at) * half_width, half_width, rows.ndim - 1)
        return from_peer(other, "dp")

    allowed = (key_positions[None, :] <= positions[:, None]) & (
        all_docs[None, :] == doc_ids[0][:, None]
    )
    allowed = allowed[:, None, :]
    score_scale = (NOPE + ROPE) ** (-0.5)
    scores = (
        jnp.einsum("qhd,kd->qhk", queries[0], all_keys, preferred_element_type=f32) * score_scale
    )
    score_peak = jnp.max(jnp.where(allowed, scores, -1e30), axis=-1, keepdims=True)
    weights = jnp.exp(jnp.where(allowed, scores - score_peak, -1e30))
    weight_total = jnp.sum(weights, axis=-1, keepdims=True)
    mixed_latent = (
        jnp.einsum(
            "qhk,kl->qhl",
            weights.astype(bf16),
            all_keys[:, :latent_width],
            preferred_element_type=f32,
        )
        / weight_total
    ).astype(bf16)
    head_values = (
        jnp.einsum("qhl,hlv->qhv", mixed_latent, uv_weight, preferred_element_type=f32)
        .astype(bf16)
        .reshape(seq_rows, -1)
    )
    head_part = jnp.dot(head_values, out_weight, preferred_element_type=f32)
    attention = scatter_rows(head_part, "exp")
    token_rows = lax.dynamic_slice_in_dim(local_rows, exp_at * half_rows, half_rows, 0)
    hidden = (token_rows.astype(f32) + attention).astype(bf16)
    normed = rms_scale(hidden.astype(f32), post_gain.astype(f32)).astype(bf16)
    normed_all = gather_rows(normed)

    arrived = to_slots(normed_all)
    arrived_peer = peer_half(arrived)
    logits = jnp.dot(normed_all, router_weight, preferred_element_type=f32)
    router_probs = jax.nn.softmax(logits, axis=-1)
    chosen = router_probs * member_f
    chosen_sum = jnp.sum(chosen, axis=1, keepdims=True)
    route_w = chosen / chosen_sum
    route_own = lax.dynamic_slice_in_dim(route_w, ctx_at * held, held, 1).reshape(
        ctx_count, seq_rows, held
    )
    route_own = lax.reduce_precision(jnp.moveaxis(route_own, 1, 2), 8, 7)
    slot_w = jnp.sum(jnp.where(hits, route_own[:, :, None, :], 0.0), axis=3)
    combine = jnp.where(hits, route_own[:, :, None, :], 0.0).astype(bf16).reshape(
        ctx_count, held * capacity, seq_rows
    )

    gate_pre = jnp.einsum("sjcd,jdf->sjcf", arrived, gate_weight, preferred_element_type=f32)
    up_pre = jnp.einsum("sjcd,jdf->sjcf", arrived, up_weight, preferred_element_type=f32)
    sigmoid_gate = jax.nn.sigmoid(gate_pre)
    activated = (gate_pre * sigmoid_gate * up_pre).astype(bf16)
    expert_part = jnp.einsum(
        "sjcf,jfd->sjcd", activated, down_weight, preferred_element_type=f32
    ).astype(bf16)
    moe_part = jnp.einsum(
        "sct,scd->std",
        combine,
        expert_part.reshape(ctx_count, held * capacity, model_width),
        preferred_element_type=f32,
    ).astype(bf16)
    moe_part, cot_all = lax.optimization_barrier((moe_part, cot_all))
    moe = lax.psum_scatter(
        moe_part.reshape(-1, model_width), ("ctx", "exp"), scatter_dimension=0, tiled=True
    )

    cot_slots = to_slots(cot_all)
    cot_peer = peer_half(cot_slots)
    dact_raw = jnp.einsum("sjcd,jfd->sjcf", cot_slots, down_weight, preferred_element_type=f32)
    weighted = (activated.astype(f32) * slot_w[..., None]).astype(bf16)
    dact = dact_raw * slot_w[..., None]
    dgate = (dact * up_pre * sigmoid_gate * (1.0 + gate_pre * (1.0 - sigmoid_gate))).astype(bf16)
    dup = (dact * gate_pre * sigmoid_gate).astype(bf16)
    weighted_peer, dgate_peer, dup_peer = (
        from_peer(weighted, "dp"),
        from_peer(dgate, "dp"),
        from_peer(dup, "dp"),
    )

    dweight_slot = jnp.sum(activated.astype(f32) * dact_raw, axis=-1)
    dweight_part = jnp.sum(jnp.where(hits, dweight_slot[..., None], 0.0), axis=2)
    dweight_part = jnp.moveaxis(dweight_part, 1, 0).reshape(held, -1)
    dweight = in_order(*gather_pairs(sum_over(dweight_part, "exp"), "ctx"))
    dweight = dweight.reshape(experts_all, -1).T
    mean_term = jnp.sum(dweight * route_w, axis=1, keepdims=True)
    dprobs = member_f * (dweight - mean_term) / chosen_sum
    dlogits = router_probs * (dprobs - jnp.sum(router_probs * dprobs, axis=1, keepdims=True))
    router_parts = jnp.einsum(
        "td,te->de", normed_all, split_parts(dlogits), preferred_element_type=f32
    )
    router_term = jnp.sum(router_parts.reshape(model_width, 3, experts_all), axis=1)
    router_grad = router_term + from_peer(router_term, "dp")

    def summed(form, own, own_other, peer, peer_other):
        first = jnp.einsum(form, own, own_other, preferred_element_type=f32)
        second = jnp.einsum(form, peer, peer_other, preferred_element_type=f32)
        return (first + second).astype(bf16)

    arrived_own = own_half(arrived)
    gate_out = summed("sjcd,sjcf->jdf", arrived_own, dgate, arrived_peer, dgate_peer)
    up_out = summed("sjcd,sjcf->jdf", arrived_own, dup, arrived_peer, dup_peer)
    down_out = summed("sjcf,sjcd->jfd", weighted, own_half(cot_slots), weighted_peer, cot_peer)

    layer_half = (hidden.astype(f32) + moe.astype(f32)).astype(bf16)
    if lax.axis_size("exp") == 2:
        other_half = from_peer(layer_half, "exp")
        layer_out = jnp.concatenate(
            [
                jnp.where(exp_at == 0, layer_half, other_half),
                jnp.where(exp_at == 0, other_half, layer_half),
            ],
            axis=0,
        )
    else:
        layer_out = lax.all_gather(layer_half, "exp", axis=0, tiled=True)
    return (layer_out[None], router_grad, gate_out, up_out, down_out)


def solution(mesh):
    placed = (
        P("dp", "ctx", None),
        P("dp", "ctx", "exp", None),
        P("exp", None),
        P(),
        P("exp", None, None),
        P("exp", None),
        P(),
        P(),
        P("dp", "ctx", None),
        P("dp", "ctx"),
        P("ctx", None, "exp"),
        P("ctx", None, "exp"),
        P("ctx", "exp", None),
        P("dp", "ctx", None),
    )
    return jax.shard_map(
        local,
        mesh=mesh,
        in_specs=placed,
        out_specs=(
            P("dp", "ctx", None),
            P(),
            P("ctx", "dp", "exp"),
            P("ctx", "dp", "exp"),
            P("ctx", "exp", "dp"),
        ),
        check_vma=False,
    )
```
